32 devices in a mesh: sx: 4 (over y, x), sz: 8 (over z, core).
Axes of the slice: x: 2, y: 2, z: 4, core: 2. Of those that a mesh axis runs over, the one named last changes fastest.
Arguments:
- right_side: float32 [72, 256, 4096], P('sx', 'sz'), may hold values from -6 to 6
- coupling: bfloat16 [72, 5, 256, 256], P('sx'), may hold values from -0.15625 to 0.15625
- harmonic_offsets: int32 [5], replicated, may hold values from -6 to 6, as said below
- eigen_basis: bfloat16 [256, 256], replicated, may hold values from -0.375 to 0.375
- eigen_inverse: bfloat16 [256, 256], replicated, may hold values from -0.375 to 0.375
- eigen_size: float32 [256], replicated, may hold values from 0.5 to 50
Outputs:
- solution: float32 [72, 256, 4096], P('sx', 'sz')
The draws below stay inside these ranges and needn't reach their ends.
Inputs may be any that keep to these rules, and one draw needn't show every extreme that they name: `harmonic_offsets`: the offsets are distinct; some offset equals 6 and some equals -6.
All inputs are finite; a program needn't handle non-finite values.
Results may differ from the reference program's by a relative error of at most 0.00065.
The reference program's roundings to bfloat16 on the way (of `rounded`, `scaled` and `search`) count: a program that leaves them out, or rounds other values in their place, can miss the bound.
Values may be sent and summed in bfloat16 or wider, within the bound.
No kernel may reach another device: no remote copies, remote signals or barrier semaphores. Data moves between devices by JAX's collectives and lax.ppermute only.
A program may use at most 192 MiB of HBM per device.

```python
import math
import jax
import jax.numpy as jnp
from jax import lax

KX = 72
KZ = 128
NC = 256
H = 5
OFF = 6
STEPS = 2
R = 32


def draw_harmonic_offsets(key, part):
    pick_key = jax.random.fold_in(key, 11)
    order_key = jax.random.fold_in(key, 23)
    middle = jnp.arange(-OFF + 1, OFF, dtype=jnp.int32)
    picked = jax.random.permutation(pick_key, middle)[:H - 2].astype(jnp.int32)
    ends = jnp.array([OFF, -OFF], dtype=jnp.int32)
    whole = jnp.concatenate([ends, picked])
    order = jax.random.permutation(order_key, H)
    return whole[order].astype(jnp.int32)


def shard_levels(key, extent, split, smallest, largest):
    def one(position, blocks):
        heights = jax.random.uniform(jax.random.fold_in(jax.random.fold_in(key, 6), position), (blocks,), jnp.float32, smallest / len(split), largest / len(split))
        return jnp.repeat(jnp.exp(heights), extent[position] // blocks).reshape((-1,) + (1,) * (len(extent) - position - 1))

    gain = one(*split[0])
    for cut in split[1:]:
        gain = gain * one(*cut)
    return gain


def scatter_about(key, extent, deviation, bound, split=(), held_as=jnp.bfloat16):
    entries = jax.random.normal(key, extent, jnp.float32) * deviation
    if len(split) > 0:
        entries = shard_levels(key, extent, split, -0.22, 0.18) * entries
    return jnp.clip(entries, min=-bound, max=bound).astype(held_as)


def setup_inputs(seed: int = 0) -> dict:
    key_list = jax.random.split(jax.random.key(seed), 7)
    right_side = scatter_about(key_list[0], (KX, NC, KZ * R), 1.0, 6.0, ((0, 4), (1, 8)), jnp.float32)
    coupling = scatter_about(key_list[1], (KX, H, NC, NC), (H * NC) ** -0.5, 0.15625, ((0, 4),))
    harmonic_offsets = draw_harmonic_offsets(jax.random.fold_in(key_list[6], 71), 0)
    eigen_basis = scatter_about(key_list[3], (NC, NC), NC ** -0.5, 0.375)
    eigen_inverse = scatter_about(key_list[4], (NC, NC), NC ** -0.5, 0.375)
    eigen_size = jnp.clip(jnp.exp(jax.random.uniform(key_list[5], (NC,), jnp.float32, math.log(0.5), math.log(50.0))), 0.5, 50.0)
    return {"right_side": right_side, "coupling": coupling, "harmonic_offsets": harmonic_offsets, "eigen_basis": eigen_basis, "eigen_inverse": eigen_inverse, "eigen_size": eigen_size}


def wave_grid():
    modes = jnp.arange(KX, dtype=jnp.int32)
    spans = jnp.arange(KZ, dtype=jnp.int32)
    signed_x = jnp.where(modes < KX // 2, modes, modes - KX).astype(jnp.float32) * (4.0 / KX)
    signed_z = jnp.where(spans < KZ // 2, spans, spans - KZ).astype(jnp.float32) * (4.0 / KZ)
    table = 1.0 + signed_x[:, None] ** 2 + signed_z[None, :] ** 2
    return jnp.repeat(table, R, axis=1)


def reference(right_side, coupling, harmonic_offsets, eigen_basis, eigen_inverse, eigen_size):
    wave_square = wave_grid()

    def precond_mode(pair):
        res_mode, wave_mode = pair
        rounded = res_mode.astype(jnp.bfloat16)
        spectral = jnp.dot(eigen_inverse, rounded, preferred_element_type=jnp.float32)
        factor = -1.0 / (eigen_size[:, None] + wave_mode[None, :])
        scaled = (spectral * factor).astype(jnp.bfloat16)
        result = jnp.dot(eigen_basis, scaled, preferred_element_type=jnp.float32)
        return result.astype(jnp.bfloat16)

    residual = right_side
    solution = jnp.zeros_like(right_side)
    for sweep in range(STEPS):
        search = lax.map(precond_mode, (residual, wave_square))

        def apply_mode(mode):
            wave_mode = lax.dynamic_index_in_dim(wave_square, mode, 0, keepdims=False)
            own = lax.dynamic_index_in_dim(search, mode, 0, keepdims=False)
            accum = -wave_mode[None, :] * own.astype(jnp.float32)
            blocks = lax.dynamic_index_in_dim(coupling, mode, 0, keepdims=False)
            for harmonic in range(H):
                target = ((mode + harmonic_offsets[harmonic]) % KX).astype(jnp.int32)
                source = lax.dynamic_index_in_dim(search, target, 0, keepdims=False)
                accum = accum + jnp.dot(blocks[harmonic], source, preferred_element_type=jnp.float32)
            return accum

        image = lax.map(apply_mode, jnp.arange(KX, dtype=jnp.int32))
        aligned = jnp.sum(jnp.sum(image * residual, axis=(0, 1)).reshape(KZ, R), axis=0)
        energy = jnp.sum(jnp.sum(image * image, axis=(0, 1)).reshape(KZ, R), axis=0)
        step_size = jnp.tile(aligned / (energy + 1e-6), KZ)
        solution = solution + step_size * search.astype(jnp.float32)
        residual = residual - step_size * image
    return solution
```

```python
import functools
import jax
import jax.numpy as jnp
from jax import lax
from jax.experimental import pallas as pl
from jax.experimental.pallas import tpu as pltpu
from jax.sharding import PartitionSpec as P

KX = 72
KZ = 128
H = 5
OFF = 6
R = 32
CHUNKS = ((0, 16), (16, 16))
F32 = jnp.float32
BF16 = jnp.bfloat16
TOP = 2.0**14
UNIT = 2.0**23
STEP = 3
VMEM = 24 * 2**20


class Order:
    def __init__(self):
        self.token = jnp.zeros((8, 128), F32)


def call(order, body, grid, in_specs, out_specs, out_shape, flops, moved, scratch=(), scalars=0):
    outs = len(out_shape)
    inputs = len(in_specs)

    def ordered(*refs):
        before, held, rest = refs[:scalars], refs[scalars : scalars + inputs], refs[scalars + inputs + 1 :]
        rest[outs][...] = jnp.zeros((8, 128), F32)
        body(*before, *held, *rest[:outs], *rest[outs + 1 :])

    kernel = pl.pallas_call(
        ordered,
        grid_spec=pltpu.PrefetchScalarGridSpec(
            num_scalar_prefetch=scalars,
            grid=grid,
            in_specs=in_specs + [pl.BlockSpec(memory_space=pl.ANY)],
            out_specs=out_specs + [whole((8, 128))],
            scratch_shapes=list(scratch),
        ),
        out_shape=out_shape + [jax.ShapeDtypeStruct((8, 128), F32)],
        compiler_params=pltpu.CompilerParams(vmem_limit_bytes=VMEM),
        cost_estimate=pl.CostEstimate(flops=int(flops), bytes_accessed=int(moved), transcendentals=0),
    )

    def run(*args):
        *given, order.token = kernel(*args, order.token)
        return given if outs > 1 else given[0]

    return run


def whole(shape):
    return pl.BlockSpec(shape, lambda m, *_: (0,) * len(shape))


def by_mode(shape, axis=0):
    return pl.BlockSpec(shape, lambda m, *_: (0,) * axis + (m,) + (0,) * (len(shape) - axis - 1))


def dot(a, b):
    return jnp.dot(a, b, preferred_element_type=F32)


def pack_body(parts, x_ref, *refs):
    picks, outs = refs[: len(parts)], refs[len(parts) :]
    modes, rows, columns = x_ref.shape
    width = picks[0].shape[0]
    peers = columns // width
    blocks = [x_ref[m, :, p * width : (p + 1) * width] for p in range(peers) for m in range(modes)]
    value = jnp.concatenate(blocks, axis=0)
    high = value.astype(BF16)
    if any(parts):
        wide = high.astype(F32)
        ratio = (value - wide) / jnp.where(wide == 0.0, 1.0, wide)
        code = jnp.clip(jnp.round(ratio * UNIT), -32767.0, 32767.0)
        upper = jnp.round(code * (1.0 / 256.0))
        lower = (code - upper * 256.0).astype(BF16)
        upper = upper.astype(BF16)
    for part, pick_ref, out_ref in zip(parts, picks, outs):
        if part:
            moved = dot(upper, pick_ref[...]) * 256.0 + dot(lower, pick_ref[...])
            moved = moved.astype(jnp.int32).astype(jnp.int16)
        else:
            moved = dot(high, pick_ref[...]).astype(BF16)
        for peer in range(peers):
            for mode in range(modes):
                at = (peer * modes + mode) * rows
                out_ref[peer, mode] = moved[at : at + rows]


def pack(order, right_side, picks, parts, peers):
    count, rows, columns = right_side.shape
    outs = [(peers, STEP, rows, pick.shape[1]) for pick in picks]
    kinds = [jnp.int16 if part else BF16 for part in parts]
    made = call(
        order,
        functools.partial(pack_body, parts),
        (count // STEP,),
        [by_mode((STEP, rows, columns))] + [whole(pick.shape) for pick in picks],
        [by_mode(shape, 1) for shape in outs],
        [jax.ShapeDtypeStruct((p, count, r, w), kind) for (p, _, r, w), kind in zip(outs, kinds)],
        2 * count * rows * columns * sum(pick.shape[1] * (1 + part) for pick, part in zip(picks, parts)),
        count * rows * columns * 4 + sum(2 * peers * count * rows * pick.shape[1] for pick in picks),
    )(right_side, *picks)
    return made if len(parts) > 1 else [made]


def pick_matrix(spans, first, amount):
    source = jnp.arange(spans * R, dtype=jnp.int32)[:, None]
    target = jnp.arange(spans * amount, dtype=jnp.int32)[None, :]
    wanted = (target // amount) * R + first + target % amount
    return (source == wanted).astype(BF16)


def gate_body(value_ref, token_ref, out_ref, next_ref):
    next_ref[...] = jnp.zeros((8, 128), F32)


def gate(order, value):
    far = pl.BlockSpec(memory_space=pl.ANY)
    value, order.token = pl.pallas_call(
        gate_body,
        in_specs=[far, far],
        out_specs=[far, pl.BlockSpec(memory_space=pltpu.VMEM)],
        out_shape=[jax.ShapeDtypeStruct(value.shape, value.dtype), jax.ShapeDtypeStruct((8, 128), F32)],
        input_output_aliases={0: 0},
    )(value, order.token)
    return value


def fold(payload, amount):
    width = payload.shape[1]
    row = lax.broadcasted_iota(jnp.int32, (width, width), 0)
    column = lax.broadcasted_iota(jnp.int32, (width, width), 1)
    same = ((row & (amount - 1)) == (column & (amount - 1))).astype(F32).astype(BF16)
    high = payload.astype(BF16)
    payload = payload - high.astype(F32)
    middle = payload.astype(BF16)
    low = (payload - middle.astype(F32)).astype(BF16)
    return dot(high, same) + (dot(middle, same) + dot(low, same))


def step_size(total):
    return total[0:1] / (total[1:2] + 1e-06)


def ceiling(first_total, second_total):
    reach = jnp.abs(step_size(first_total)) * jnp.sqrt(first_total[2:3])
    reach = reach + jnp.abs(step_size(second_total)) * jnp.sqrt(second_total[2:3])
    return jnp.maximum(jnp.max(reach, axis=1, keepdims=True), 1e-30)


def fold_rows(value):
    return jnp.sum(value.reshape(-1, 8, value.shape[-1]), axis=0)


def column_sum(value):
    return jnp.sum(value, axis=0, keepdims=True)


def is_first():
    return pl.program_id(0) == 0


def is_last():
    return pl.program_id(0) == pl.num_programs(0) - 1


def zero(ref):
    @pl.when(is_first())
    def _():
        ref[...] = jnp.zeros_like(ref)


def direction(rounded, wave, inverse_ref, basis_ref, size_ref):
    spectral = dot(inverse_ref[...], rounded)
    scaled = (spectral * (-1.0 / (size_ref[...] + wave))).astype(BF16)
    return dot(basis_ref[...], scaled).astype(BF16)


def hand_out(searches, search_ref, first_ref, last_ref, norm_ref, norm_scratch):
    at = pl.program_id(0)
    edge = OFF // STEP
    zero(norm_scratch)
    for i, search in enumerate(searches):
        search_ref[i] = search
        wide = search.astype(F32)
        norm_scratch[...] += fold_rows(wide * wide)

    @pl.when(at < edge)
    def _():
        for i, search in enumerate(searches):
            first_ref[i] = search

    @pl.when(at >= pl.num_programs(0) - edge)
    def _():
        for i, search in enumerate(searches):
            last_ref[i] = search

    @pl.when(is_last())
    def _():
        norm_ref[...] = norm_scratch[...]


def begin_body(high_ref, inverse_ref, basis_ref, size_ref, wave_ref, *outs):
    points = inverse_ref.shape[0]
    searches = []
    for i in range(STEP):
        rounded = high_ref[:, i].reshape(points, -1)
        searches.append(direction(rounded, wave_ref[i], inverse_ref, basis_ref, size_ref))
    hand_out(searches, *outs)


def edge_specs(count, points, width):
    shape = (STEP, points, width)
    edge = OFF // STEP
    first = pl.BlockSpec(shape, lambda m, *_: (jnp.minimum(m, edge - 1), 0, 0))
    last = pl.BlockSpec(shape, lambda m, *_: (jnp.maximum(m - (count // STEP - edge), 0), 0, 0))
    return [by_mode(shape), first, last, whole((8, width))]


def edge_shapes(count, points, width):
    shapes = [(count, points, width), (OFF, points, width), (OFF, points, width)]
    return [jax.ShapeDtypeStruct(s, BF16) for s in shapes] + [jax.ShapeDtypeStruct((8, width), F32)]


def begin(order, high, inverse, basis, size, wave):
    peers, count, rows, width = high.shape
    points = peers * rows
    return call(
        order,
        begin_body,
        (count // STEP,),
        [by_mode((peers, STEP, rows, width), 1), whole(inverse.shape), whole(basis.shape), whole(size.shape), by_mode((STEP, 1, width))],
        edge_specs(count, points, width),
        edge_shapes(count, points, width),
        4 * count * points * points * width,
        4 * count * points * width,
        scratch=[pltpu.VMEM((8, width), F32)],
    )(high, inverse, basis, size, wave)


def removed(high_ref, low_ref, i):
    high = high_ref[:, i].astype(F32)
    return (high * (1.0 / UNIT)) * low_ref[:, i].astype(jnp.int32).astype(F32)


def again_body(amount, high_ref, low_ref, image_ref, total_ref, inverse_ref, basis_ref, size_ref, wave_ref, residual_ref, *rest):
    outs, step_ref = rest[:-1], rest[-1]
    points = inverse_ref.shape[0]

    @pl.when(is_first())
    def _():
        step_ref[0:1] = step_size(fold(total_ref[...], amount))

    searches = []
    for i in range(STEP):
        held = high_ref[:, i].astype(F32) + removed(high_ref, low_ref, i)
        residual = held.reshape(points, -1) - step_ref[0:1] * image_ref[i]
        residual_ref[i] = residual
        searches.append(direction(residual.astype(BF16), wave_ref[i], inverse_ref, basis_ref, size_ref))
    hand_out(searches, *outs)


def again(order, amount, high, low, image, total, inverse, basis, size, wave):
    peers, count, rows, width = high.shape
    points = peers * rows
    block = by_mode((peers, STEP, rows, width), 1)
    plane = by_mode((STEP, points, width))
    return call(
        order,
        functools.partial(again_body, amount),
        (count // STEP,),
        [block, block, plane, whole(total.shape), whole(inverse.shape), whole(basis.shape), whole(size.shape), by_mode((STEP, 1, width))],
        [plane] + edge_specs(count, points, width),
        [jax.ShapeDtypeStruct((count, points, width), F32)] + edge_shapes(count, points, width),
        4 * count * points * points * width,
        14 * count * points * width,
        scratch=[pltpu.VMEM((8, width), F32), pltpu.VMEM((8, width), F32)],
    )(high, low, image, total, inverse, basis, size, wave)


def bring(before_ref, search_ref, after_ref, padded_ref, arrived):
    count = search_ref.shape[0]

    @pl.when(is_first())
    def _():
        parts = [
            pltpu.make_async_copy(before_ref, padded_ref.at[pl.ds(0, OFF)], arrived.at[0]),
            pltpu.make_async_copy(search_ref, padded_ref.at[pl.ds(OFF, count)], arrived.at[1]),
            pltpu.make_async_copy(after_ref, padded_ref.at[pl.ds(OFF + count, OFF)], arrived.at[2]),
        ]
        for part in parts:
            part.start()
        for part in parts:
            part.wait()


def operate(i, offsets_ref, coupling_ref, wave_ref, padded_ref):
    mode = pl.program_id(0) * STEP + i
    blocks = jnp.concatenate([coupling_ref[i, h] for h in range(H)], axis=1)
    sources = jnp.concatenate([padded_ref[mode + OFF + offsets_ref[h]] for h in range(H)], axis=0)
    return dot(blocks, sources) - wave_ref[i] * padded_ref[mode + OFF].astype(F32)


def apply_body(offsets_ref, before_ref, search_ref, after_ref, coupling_ref, wave_ref, high_ref, image_ref, sums_ref, padded_ref, arrived, sums):
    bring(before_ref, search_ref, after_ref, padded_ref, arrived)
    zero(sums)
    for i in range(STEP):
        image = operate(i, offsets_ref, coupling_ref, wave_ref, padded_ref)
        image_ref[i] = image
        sums[0:8] += fold_rows(image * high_ref[:, i].reshape(image.shape).astype(F32))
        sums[8:16] += fold_rows(image * image)

    @pl.when(is_last())
    def _():
        sums_ref[...] = jnp.zeros_like(sums_ref)
        sums_ref[0:1] = column_sum(sums[0:8])
        sums_ref[1:2] = column_sum(sums[8:16])


def apply_last_body(offsets_ref, before_ref, search_ref, after_ref, coupling_ref, wave_ref, residual_ref, norm_ref, sums_ref, padded_ref, arrived, sums):
    bring(before_ref, search_ref, after_ref, padded_ref, arrived)
    zero(sums)
    for i in range(STEP):
        image = operate(i, offsets_ref, coupling_ref, wave_ref, padded_ref)
        sums[0:8] += fold_rows(image * residual_ref[i])
        sums[8:16] += fold_rows(image * image)

    @pl.when(is_last())
    def _():
        sums_ref[...] = jnp.zeros_like(sums_ref)
        sums_ref[0:1] = column_sum(sums[0:8])
        sums_ref[1:2] = column_sum(sums[8:16])
        sums_ref[2:3] = column_sum(norm_ref[...])


def operator_specs(points, width):
    far = pl.BlockSpec(memory_space=pl.ANY)
    return [far, far, far, by_mode((STEP, H, points, points)), by_mode((STEP, 1, width))]


def operator_scratch(count, points, width):
    return [pltpu.VMEM((count + 2 * OFF, points, width), BF16), pltpu.SemaphoreType.DMA((3,)), pltpu.VMEM((16, width), F32)]


def apply(order, offsets, before, search, after, coupling, wave, high):
    count, points, width = search.shape
    peers, _, rows, _ = high.shape
    return call(
        order,
        apply_body,
        (count // STEP,),
        operator_specs(points, width) + [by_mode((peers, STEP, rows, width), 1)],
        [by_mode((STEP, points, width)), whole((8, width))],
        [jax.ShapeDtypeStruct((count, points, width), F32), jax.ShapeDtypeStruct((8, width), F32)],
        2 * H * count * points * points * width,
        2 * count * points * (H * points + 5 * width),
        scratch=operator_scratch(count, points, width),
        scalars=1,
    )(offsets, before, search, after, coupling, wave, high)


def apply_last(order, offsets, before, search, after, coupling, wave, residual, norm):
    count, points, width = search.shape
    return call(
        order,
        apply_last_body,
        (count // STEP,),
        operator_specs(points, width) + [by_mode((STEP, points, width)), whole(norm.shape)],
        [whole((8, width))],
        [jax.ShapeDtypeStruct((8, width), F32)],
        2 * H * count * points * points * width,
        2 * count * points * (H * points + 3 * width),
        scratch=operator_scratch(count, points, width),
        scalars=1,
    )(offsets, before, search, after, coupling, wave, residual, norm)


def rest_body(image_ref, high_ref, low_ref, sums_ref, norm_ref, out_ref, sums):
    zero(sums)
    for i in range(STEP):
        image = image_ref[i]
        sums[...] += fold_rows(image * removed(high_ref, low_ref, i).reshape(image.shape))

    @pl.when(is_last())
    def _():
        out_ref[...] = sums_ref[...]
        out_ref[0:1] += column_sum(sums[...])
        out_ref[2:3] = column_sum(norm_ref[...])


def rest(order, image, high, low, sums, norm):
    count, points, width = image.shape
    peers, _, rows, _ = low.shape
    return call(
        order,
        rest_body,
        (count // STEP,),
        [by_mode((STEP, points, width))] + [by_mode((peers, STEP, rows, width), 1)] * 2 + [whole(sums.shape), whole(norm.shape)],
        [whole((8, width))],
        [jax.ShapeDtypeStruct((8, width), F32)],
        2 * count * points * width,
        8 * count * points * width,
        scratch=[pltpu.VMEM((8, width), F32)],
    )(image, high, low, sums, norm)


def combine_body(amount, one_ref, two_ref, first_ref, second_ref, out_ref, step_ref):
    @pl.when(pl.program_id(0) == 0)
    def _():
        first_total = fold(first_ref[...], amount)
        second_total = fold(second_ref[...], amount)
        step_ref[0:1] = step_size(first_total)
        step_ref[1:2] = step_size(second_total)
        step_ref[2:3] = jnp.broadcast_to(TOP / ceiling(first_total, second_total), (1, step_ref.shape[1]))

    for i in range(STEP):
        value = step_ref[0:1] * one_ref[i].astype(F32) + step_ref[1:2] * two_ref[i].astype(F32)
        out_ref[:, i] = (value * step_ref[2:3]).reshape(out_ref.shape[0], out_ref.shape[2], -1)


def combine(order, amount, one, two, first_total, second_total, peers):
    count, points, width = one.shape
    rows = points // peers
    plane = by_mode((STEP, points, width))
    return call(
        order,
        functools.partial(combine_body, amount),
        (count // STEP,),
        [plane, plane, whole((8, width)), whole((8, width))],
        [by_mode((peers, STEP, rows, width), 1)],
        [jax.ShapeDtypeStruct((peers, count, rows, width), F32)],
        4 * count * points * width,
        8 * count * points * width,
        scratch=[pltpu.VMEM((8, width), F32)],
    )(one, two, first_total, second_total)


def spread_body(*refs):
    amounts = [amount for _, amount in CHUNKS]
    n = len(amounts)
    values, firsts, seconds = refs[:n], refs[n : 2 * n], refs[2 * n : 3 * n]
    place_ref, out_ref, scale_ref = refs[3 * n :]
    peers, modes, rows, _ = values[0].shape
    width = place_ref.shape[1]

    @pl.when(pl.program_id(0) == 0)
    def _():
        side = lax.broadcasted_iota(jnp.int32, (1, width), 1) & (R - 1)
        scale = jnp.zeros((1, width), F32)
        for (first, amount), one_ref, two_ref in zip(CHUNKS, firsts, seconds):
            top = ceiling(fold(one_ref[...], amount), fold(two_ref[...], amount)) * (1.0 / TOP)
            scale = jnp.where((side >= first) & (side < first + amount), top, scale)
        scale_ref[0:1] = scale

    joined = jnp.concatenate([v[...].reshape(peers * modes * rows, v.shape[3]) for v in values], axis=1)
    high = joined.astype(BF16)
    low = (joined - high.astype(F32)).astype(BF16)
    moved = (dot(high, place_ref[...]) + dot(low, place_ref[...])) * scale_ref[0:1]
    for peer in range(peers):
        for mode in range(modes):
            at = (peer * modes + mode) * rows
            out_ref[mode, :, peer * width : (peer + 1) * width] = moved[at : at + rows]


def spread(order, values, firsts, seconds, place):
    peers, count, rows, _ = values[0].shape
    step = STEP
    width = place.shape[1]
    columns = peers * width
    return call(
        order,
        spread_body,
        (count // step,),
        [by_mode((peers, step, rows, v.shape[3]), 1) for v in values]
        + [whole(t.shape) for t in firsts + seconds]
        + [whole(place.shape)],
        [by_mode((step, rows, columns))],
        [jax.ShapeDtypeStruct((count, rows, columns), F32)],
        4 * count * rows * columns * width,
        8 * count * rows * columns,
        scratch=[pltpu.VMEM((8, width), F32)],
    )(*values, *firsts, *seconds, place)


def swap(value):
    return lax.all_to_all(value, "sz", split_axis=0, concat_axis=0, tiled=True)


def edges(first, last):
    peers = lax.axis_size("sx")
    up = [(i, (i + 1) % peers) for i in range(peers)]
    down = [(j, i) for i, j in up]
    return lax.ppermute(last, "sx", up), lax.ppermute(first, "sx", down)


def exchange(value, axis, distance):
    return lax.ppermute(value, axis, [(i, i ^ distance) for i in range(lax.axis_size(axis))])


def total_span(value):
    value = value + exchange(value, "sz", 1)
    return sum([exchange(value, "sz", d) for d in range(2, lax.axis_size("sz"), 2)], value)


def total_mode(value):
    distance = 1
    while distance < lax.axis_size("sx"):
        value = value + exchange(value, "sx", distance)
        distance *= 2
    return value


def wave_table(mode_count, span_count, amount):
    first_mode = lax.axis_index("sx") * mode_count
    first_span = lax.axis_index("sz") * span_count
    modes = first_mode + jnp.arange(mode_count, dtype=jnp.int32)
    spans = first_span + jnp.arange(span_count * amount, dtype=jnp.int32) // amount
    signed_x = jnp.where(modes < KX // 2, modes, modes - KX).astype(F32) * (4.0 / KX)
    signed_z = jnp.where(spans < KZ // 2, spans, spans - KZ).astype(F32) * (4.0 / KZ)
    return 1.0 + signed_x[:, None, None] ** 2 + signed_z[None, None, :] ** 2


class Chunk:
    def __init__(self, order, arrays, first, amount):
        self.order, self.amount = order, amount
        self.right_side, self.coupling, self.offsets, self.basis, self.inverse, self.size = arrays
        self.peers = lax.axis_size("sz")
        self.spans = KZ // self.peers
        self.pick = pick_matrix(self.spans, first, amount)
        self.wave = wave_table(self.right_side.shape[0], self.spans, amount)

    def send_high(self):
        self.high = swap(self.high)

    def send_low(self):
        self.low = swap(self.low)

    def gate_high(self):
        self.high = swap(gate(self.order, self.high))

    def gate_low(self):
        self.low = swap(gate(self.order, self.low))

    def begin(self):
        self.one, first, last, self.norm = begin(self.order, self.high, self.inverse, self.basis, self.size, self.wave)
        self.before, self.after = edges(first, last)

    def apply(self):
        self.image, self.sums = apply(
            self.order, self.offsets, self.before, self.one, self.after, self.coupling, self.wave, self.high
        )

    def rest(self):
        spans = total_span(rest(self.order, self.image, self.high, self.low, self.sums, self.norm))
        self.order.token = spans
        self.first = total_mode(spans)

    def again(self):
        self.residual, self.two, first, last, self.norm = again(
            self.order, self.amount, self.high, self.low, self.image, self.first, self.inverse, self.basis, self.size, self.wave
        )
        self.before, self.after = edges(first, last)

    def finish(self):
        sums = apply_last(
            self.order, self.offsets, self.before, self.two, self.after, self.coupling, self.wave, self.residual, self.norm
        )
        self.second = total_mode(total_span(sums))

    def combine(self):
        sent = combine(self.order, self.amount, self.one, self.two, self.first, self.second, self.peers)
        self.value = swap(sent.astype(jnp.float16)).astype(F32)


PLAN = (
    "send_high0 send_low0 begin0 apply0 rest0 gate_high1 again0 gate_low1 begin1 finish0 "
    "apply1 rest1 combine0 again1 finish1 combine1"
)


def shards(right_side, coupling, offsets, basis, inverse, size):
    order = Order()
    arrays = (right_side, coupling, offsets, basis, inverse, size[:, None])
    chunks = [Chunk(order, arrays, first, amount) for first, amount in CHUNKS]
    peers = chunks[0].peers
    chunks[0].high, = pack(order, right_side, [chunks[0].pick], (0,), peers)
    others = [(chunks[0], 1)] + [(chunk, part) for chunk in chunks[1:] for part in (0, 1)]
    made = pack(order, right_side, [chunk.pick for chunk, _ in others], tuple(part for _, part in others), peers)
    for (chunk, part), value in zip(others, made):
        setattr(chunk, "low" if part else "high", value)
    for step in PLAN.split():
        getattr(chunks[int(step[-1])], step[:-1])()
    place = jnp.concatenate([c.pick.T for c in chunks], axis=0)
    return spread(order, [c.value for c in chunks], [c.first for c in chunks], [c.second for c in chunks], place)


def solution(mesh):
    in_specs = (P("sx", "sz", None), P("sx", None, None, None), P(), P(), P(), P())
    out_specs = P("sx", "sz", None)
    return jax.shard_map(shards, mesh=mesh, in_specs=in_specs, out_specs=out_specs, check_vma=False)
```

```python
import functools
import jax
import jax.numpy as jnp
from jax import lax
from jax.experimental import pallas as pl
from jax.experimental.pallas import tpu as pltpu
from jax.sharding import PartitionSpec as P

KX = 72
KZ = 128
H = 5
OFF = 6
R = 32
CHUNKS = ((0, 16), (16, 16))
F32 = jnp.float32
BF16 = jnp.bfloat16
TOP = 2.0**14
UNIT = 2.0**23
STEP = 3
VMEM = 24 * 2**20


class Order:
    def __init__(self):
        self.token = jnp.zeros((8, 128), F32)


def call(order, body, grid, in_specs, out_specs, out_shape, flops, moved, scratch=(), scalars=0, grant=VMEM):
    outs = len(out_shape)
    inputs = len(in_specs)

    def ordered(*refs):
        before, held, rest = refs[:scalars], refs[scalars : scalars + inputs], refs[scalars + inputs + 1 :]
        rest[outs][...] = jnp.zeros((8, 128), F32)
        body(*before, *held, *rest[:outs], *rest[outs + 1 :])

    kernel = pl.pallas_call(
        ordered,
        grid_spec=pltpu.PrefetchScalarGridSpec(
            num_scalar_prefetch=scalars,
            grid=grid,
            in_specs=in_specs + [pl.BlockSpec(memory_space=pl.ANY)],
            out_specs=out_specs + [whole((8, 128))],
            scratch_shapes=list(scratch),
        ),
        out_shape=out_shape + [jax.ShapeDtypeStruct((8, 128), F32)],
        compiler_params=pltpu.CompilerParams(vmem_limit_bytes=grant),
        cost_estimate=pl.CostEstimate(flops=int(flops), bytes_accessed=int(moved), transcendentals=0),
    )

    def run(*args):
        *given, order.token = kernel(*args, order.token)
        return given if outs > 1 else given[0]

    return run


def whole(shape):
    return pl.BlockSpec(shape, lambda m, *_: (0,) * len(shape))


def by_mode(shape, axis=0):
    return pl.BlockSpec(shape, lambda m, *_: (0,) * axis + (m,) + (0,) * (len(shape) - axis - 1))


def dot(a, b):
    return jnp.dot(a, b, preferred_element_type=F32)


def pack_body(parts, x_ref, *refs):
    picks, outs = refs[: len(parts)], refs[len(parts) :]
    modes, rows, columns = x_ref.shape
    width = picks[0].shape[0]
    peers = columns // width
    blocks = [x_ref[m, :, p * width : (p + 1) * width] for p in range(peers) for m in range(modes)]
    value = jnp.concatenate(blocks, axis=0)
    high = value.astype(BF16)
    if any(parts):
        wide = high.astype(F32)
        ratio = (value - wide) / jnp.where(wide == 0.0, 1.0, wide)
        code = jnp.clip(jnp.round(ratio * UNIT), -32767.0, 32767.0)
        upper = jnp.round(code * (1.0 / 256.0))
        lower = (code - upper * 256.0).astype(BF16)
        upper = upper.astype(BF16)
    for part, pick_ref, out_ref in zip(parts, picks, outs):
        if part:
            moved = dot(upper, pick_ref[...]) * 256.0 + dot(lower, pick_ref[...])
            moved = moved.astype(jnp.int32).astype(jnp.int16)
        else:
            moved = dot(high, pick_ref[...]).astype(BF16)
        for peer in range(peers):
            for mode in range(modes):
                at = (peer * modes + mode) * rows
                out_ref[peer, mode] = moved[at : at + rows]


def pack(order, right_side, picks, parts, peers):
    count, rows, columns = right_side.shape
    outs = [(peers, STEP, rows, pick.shape[1]) for pick in picks]
    kinds = [jnp.int16 if part else BF16 for part in parts]
    made = call(
        order,
        functools.partial(pack_body, parts),
        (count // STEP,),
        [by_mode((STEP, rows, columns))] + [whole(pick.shape) for pick in picks],
        [by_mode(shape, 1) for shape in outs],
        [jax.ShapeDtypeStruct((p, count, r, w), kind) for (p, _, r, w), kind in zip(outs, kinds)],
        2 * count * rows * columns * sum(pick.shape[1] * (1 + part) for pick, part in zip(picks, parts)),
        count * rows * columns * 4 + sum(2 * peers * count * rows * pick.shape[1] for pick in picks),
    )(right_side, *picks)
    return made if len(parts) > 1 else [made]


def pick_matrix(spans, first, amount):
    source = jnp.arange(spans * R, dtype=jnp.int32)[:, None]
    target = jnp.arange(spans * amount, dtype=jnp.int32)[None, :]
    wanted = (target // amount) * R + first + target % amount
    return (source == wanted).astype(BF16)


def gate_body(value_ref, token_ref, out_ref, next_ref):
    next_ref[...] = jnp.zeros((8, 128), F32)


def gate(order, value):
    far = pl.BlockSpec(memory_space=pl.ANY)
    value, order.token = pl.pallas_call(
        gate_body,
        in_specs=[far, far],
        out_specs=[far, pl.BlockSpec(memory_space=pltpu.VMEM)],
        out_shape=[jax.ShapeDtypeStruct(value.shape, value.dtype), jax.ShapeDtypeStruct((8, 128), F32)],
        input_output_aliases={0: 0},
    )(value, order.token)
    return value


def fold(payload, amount):
    width = payload.shape[1]
    row = lax.broadcasted_iota(jnp.int32, (width, width), 0)
    column = lax.broadcasted_iota(jnp.int32, (width, width), 1)
    same = ((row & (amount - 1)) == (column & (amount - 1))).astype(F32).astype(BF16)
    high = payload.astype(BF16)
    payload = payload - high.astype(F32)
    middle = payload.astype(BF16)
    low = (payload - middle.astype(F32)).astype(BF16)
    return dot(high, same) + (dot(middle, same) + dot(low, same))


def step_size(total):
    return total[0:1] / (total[1:2] + 1e-06)


def ceiling(first_total, second_total):
    reach = jnp.abs(step_size(first_total)) * jnp.sqrt(first_total[2:3])
    reach = reach + jnp.abs(step_size(second_total)) * jnp.sqrt(second_total[2:3])
    return jnp.maximum(jnp.max(reach, axis=1, keepdims=True), 1e-30)


def fold_rows(value):
    return jnp.sum(value.reshape(-1, 8, value.shape[-1]), axis=0)


def column_sum(value):
    return jnp.sum(value, axis=0, keepdims=True)


def is_first():
    return pl.program_id(0) == 0


def is_last():
    return pl.program_id(0) == pl.num_programs(0) - 1


def zero(ref):
    @pl.when(is_first())
    def _():
        ref[...] = jnp.zeros_like(ref)


def direction(rounded, wave, inverse_ref, basis_ref, size_ref):
    spectral = dot(inverse_ref[...], rounded)
    scaled = (spectral * (-1.0 / (size_ref[...] + wave))).astype(BF16)
    return dot(basis_ref[...], scaled).astype(BF16)


def hand_out(searches, search_ref, first_ref, last_ref, norm_ref, norm_scratch):
    at = pl.program_id(0)
    edge = OFF // STEP
    zero(norm_scratch)
    for i, search in enumerate(searches):
        search_ref[i] = search
        wide = search.astype(F32)
        norm_scratch[...] += fold_rows(wide * wide)

    @pl.when(at < edge)
    def _():
        for i, search in enumerate(searches):
            first_ref[i] = search

    @pl.when(at >= pl.num_programs(0) - edge)
    def _():
        for i, search in enumerate(searches):
            last_ref[i] = search

    @pl.when(is_last())
    def _():
        norm_ref[...] = norm_scratch[...]


def begin_body(high_ref, inverse_ref, basis_ref, size_ref, wave_ref, *outs):
    points = inverse_ref.shape[0]
    searches = []
    for i in range(STEP):
        rounded = high_ref[:, i].reshape(points, -1)
        searches.append(direction(rounded, wave_ref[i], inverse_ref, basis_ref, size_ref))
    hand_out(searches, *outs)


def edge_specs(count, points, width):
    shape = (STEP, points, width)
    edge = OFF // STEP
    first = pl.BlockSpec(shape, lambda m, *_: (jnp.minimum(m, edge - 1), 0, 0))
    last = pl.BlockSpec(shape, lambda m, *_: (jnp.maximum(m - (count // STEP - edge), 0), 0, 0))
    return [by_mode(shape), first, last, whole((8, width))]


def edge_shapes(count, points, width):
    shapes = [(count, points, width), (OFF, points, width), (OFF, points, width)]
    return [jax.ShapeDtypeStruct(s, BF16) for s in shapes] + [jax.ShapeDtypeStruct((8, width), F32)]


def begin(order, high, inverse, basis, size, wave):
    peers, count, rows, width = high.shape
    points = peers * rows
    return call(
        order,
        begin_body,
        (count // STEP,),
        [by_mode((peers, STEP, rows, width), 1), whole(inverse.shape), whole(basis.shape), whole(size.shape), by_mode((STEP, 1, width))],
        edge_specs(count, points, width),
        edge_shapes(count, points, width),
        4 * count * points * points * width,
        4 * count * points * width,
        scratch=[pltpu.VMEM((8, width), F32)],
    )(high, inverse, basis, size, wave)


def removed(high_ref, low_ref, i):
    high = high_ref[:, i].astype(F32)
    return (high * (1.0 / UNIT)) * low_ref[:, i].astype(jnp.int32).astype(F32)


def again_body(amount, high_ref, low_ref, image_ref, total_ref, inverse_ref, basis_ref, size_ref, wave_ref, residual_ref, *rest):
    outs, step_ref = rest[:-1], rest[-1]
    points = inverse_ref.shape[0]

    @pl.when(is_first())
    def _():
        step_ref[0:1] = step_size(fold(total_ref[...], amount))

    searches = []
    for i in range(STEP):
        held = high_ref[:, i].astype(F32) + removed(high_ref, low_ref, i)
        residual = held.reshape(points, -1) - step_ref[0:1] * image_ref[i]
        residual_ref[i] = residual
        searches.append(direction(residual.astype(BF16), wave_ref[i], inverse_ref, basis_ref, size_ref))
    hand_out(searches, *outs)


def again(order, amount, high, low, image, total, inverse, basis, size, wave):
    peers, count, rows, width = high.shape
    points = peers * rows
    block = by_mode((peers, STEP, rows, width), 1)
    plane = by_mode((STEP, points, width))
    return call(
        order,
        functools.partial(again_body, amount),
        (count // STEP,),
        [block, block, plane, whole(total.shape), whole(inverse.shape), whole(basis.shape), whole(size.shape), by_mode((STEP, 1, width))],
        [plane] + edge_specs(count, points, width),
        [jax.ShapeDtypeStruct((count, points, width), F32)] + edge_shapes(count, points, width),
        4 * count * points * points * width,
        14 * count * points * width,
        scratch=[pltpu.VMEM((8, width), F32), pltpu.VMEM((8, width), F32)],
    )(high, low, image, total, inverse, basis, size, wave)


def bring(before_ref, search_ref, after_ref, padded_ref, arrived):
    count = search_ref.shape[0]

    @pl.when(is_first())
    def _():
        parts = [
            pltpu.make_async_copy(before_ref, padded_ref.at[pl.ds(0, OFF)], arrived.at[0]),
            pltpu.make_async_copy(search_ref, padded_ref.at[pl.ds(OFF, count)], arrived.at[1]),
            pltpu.make_async_copy(after_ref, padded_ref.at[pl.ds(OFF + count, OFF)], arrived.at[2]),
        ]
        for part in parts:
            part.start()
        for part in parts:
            part.wait()


def operate(i, offsets_ref, coupling_ref, wave_ref, padded_ref):
    mode = pl.program_id(0) * STEP + i
    blocks = jnp.concatenate([coupling_ref[i, h] for h in range(H)], axis=1)
    sources = jnp.concatenate([padded_ref[mode + OFF + offsets_ref[h]] for h in range(H)], axis=0)
    return dot(blocks, sources) - wave_ref[i] * padded_ref[mode + OFF].astype(F32)


def apply_body(offsets_ref, before_ref, search_ref, after_ref, coupling_ref, wave_ref, high_ref, image_ref, sums_ref, padded_ref, arrived, sums):
    bring(before_ref, search_ref, after_ref, padded_ref, arrived)
    zero(sums)
    for i in range(STEP):
        image = operate(i, offsets_ref, coupling_ref, wave_ref, padded_ref)
        image_ref[i] = image
        sums[0:8] += fold_rows(image * high_ref[:, i].reshape(image.shape).astype(F32))
        sums[8:16] += fold_rows(image * image)

    @pl.when(is_last())
    def _():
        sums_ref[...] = jnp.zeros_like(sums_ref)
        sums_ref[0:1] = column_sum(sums[0:8])
        sums_ref[1:2] = column_sum(sums[8:16])


def apply_last_body(offsets_ref, before_ref, search_ref, after_ref, coupling_ref, wave_ref, residual_ref, norm_ref, sums_ref, padded_ref, arrived, sums):
    bring(before_ref, search_ref, after_ref, padded_ref, arrived)
    zero(sums)
    for i in range(STEP):
        image = operate(i, offsets_ref, coupling_ref, wave_ref, padded_ref)
        sums[0:8] += fold_rows(image * residual_ref[i])
        sums[8:16] += fold_rows(image * image)

    @pl.when(is_last())
    def _():
        sums_ref[...] = jnp.zeros_like(sums_ref)
        sums_ref[0:1] = column_sum(sums[0:8])
        sums_ref[1:2] = column_sum(sums[8:16])
        sums_ref[2:3] = column_sum(norm_ref[...])


def operator_specs(points, width):
    far = pl.BlockSpec(memory_space=pl.ANY)
    return [far, far, far, by_mode((STEP, H, points, points)), by_mode((STEP, 1, width))]


def operator_scratch(count, points, width):
    return [pltpu.VMEM((count + 2 * OFF, points, width), BF16), pltpu.SemaphoreType.DMA((3,)), pltpu.VMEM((16, width), F32)]


def apply(order, offsets, before, search, after, coupling, wave, high):
    count, points, width = search.shape
    peers, _, rows, _ = high.shape
    return call(
        order,
        apply_body,
        (count // STEP,),
        operator_specs(points, width) + [by_mode((peers, STEP, rows, width), 1)],
        [by_mode((STEP, points, width)), whole((8, width))],
        [jax.ShapeDtypeStruct((count, points, width), F32), jax.ShapeDtypeStruct((8, width), F32)],
        2 * H * count * points * points * width,
        2 * count * points * (H * points + 5 * width),
        scratch=operator_scratch(count, points, width),
        scalars=1,
    )(offsets, before, search, after, coupling, wave, high)


def apply_last(order, offsets, before, search, after, coupling, wave, residual, norm):
    count, points, width = search.shape
    return call(
        order,
        apply_last_body,
        (count // STEP,),
        operator_specs(points, width) + [by_mode((STEP, points, width)), whole(norm.shape)],
        [whole((8, width))],
        [jax.ShapeDtypeStruct((8, width), F32)],
        2 * H * count * points * points * width,
        2 * count * points * (H * points + 3 * width),
        scratch=operator_scratch(count, points, width),
        scalars=1,
    )(offsets, before, search, after, coupling, wave, residual, norm)


def rest_body(image_ref, high_ref, low_ref, sums_ref, norm_ref, out_ref, sums):
    zero(sums)
    for i in range(STEP):
        image = image_ref[i]
        sums[...] += fold_rows(image * removed(high_ref, low_ref, i).reshape(image.shape))

    @pl.when(is_last())
    def _():
        out_ref[...] = sums_ref[...]
        out_ref[0:1] += column_sum(sums[...])
        out_ref[2:3] = column_sum(norm_ref[...])


def rest(order, image, high, low, sums, norm):
    count, points, width = image.shape
    peers, _, rows, _ = low.shape
    return call(
        order,
        rest_body,
        (count // STEP,),
        [by_mode((STEP, points, width))] + [by_mode((peers, STEP, rows, width), 1)] * 2 + [whole(sums.shape), whole(norm.shape)],
        [whole((8, width))],
        [jax.ShapeDtypeStruct((8, width), F32)],
        2 * count * points * width,
        8 * count * points * width,
        scratch=[pltpu.VMEM((8, width), F32)],
        grant=58 * 2**20,
    )(image, high, low, sums, norm)


def combine_body(amount, one_ref, two_ref, first_ref, second_ref, out_ref, step_ref):
    @pl.when(pl.program_id(0) == 0)
    def _():
        first_total = fold(first_ref[...], amount)
        second_total = fold(second_ref[...], amount)
        step_ref[0:1] = step_size(first_total)
        step_ref[1:2] = step_size(second_total)
        step_ref[2:3] = jnp.broadcast_to(TOP / ceiling(first_total, second_total), (1, step_ref.shape[1]))

    for i in range(STEP):
        value = step_ref[0:1] * one_ref[i].astype(F32) + step_ref[1:2] * two_ref[i].astype(F32)
        out_ref[:, i] = (value * step_ref[2:3]).reshape(out_ref.shape[0], out_ref.shape[2], -1)


def combine(order, amount, one, two, first_total, second_total, peers):
    count, points, width = one.shape
    rows = points // peers
    plane = by_mode((STEP, points, width))
    return call(
        order,
        functools.partial(combine_body, amount),
        (count // STEP,),
        [plane, plane, whole((8, width)), whole((8, width))],
        [by_mode((peers, STEP, rows, width), 1)],
        [jax.ShapeDtypeStruct((peers, count, rows, width), F32)],
        4 * count * points * width,
        8 * count * points * width,
        scratch=[pltpu.VMEM((8, width), F32)],
    )(one, two, first_total, second_total)


def spread_body(*refs):
    amounts = [amount for _, amount in CHUNKS]
    n = len(amounts)
    values, firsts, seconds = refs[:n], refs[n : 2 * n], refs[2 * n : 3 * n]
    place_ref, out_ref, scale_ref = refs[3 * n :]
    peers, modes, rows, _ = values[0].shape
    width = place_ref.shape[1]

    @pl.when(pl.program_id(0) == 0)
    def _():
        side = lax.broadcasted_iota(jnp.int32, (1, width), 1) & (R - 1)
        scale = jnp.zeros((1, width), F32)
        for (first, amount), one_ref, two_ref in zip(CHUNKS, firsts, seconds):
            top = ceiling(fold(one_ref[...], amount), fold(two_ref[...], amount)) * (1.0 / TOP)
            scale = jnp.where((side >= first) & (side < first + amount), top, scale)
        scale_ref[0:1] = scale

    joined = jnp.concatenate([v[...].reshape(peers * modes * rows, v.shape[3]) for v in values], axis=1)
    high = joined.astype(BF16)
    low = (joined - high.astype(F32)).astype(BF16)
    moved = (dot(high, place_ref[...]) + dot(low, place_ref[...])) * scale_ref[0:1]
    for peer in range(peers):
        for mode in range(modes):
            at = (peer * modes + mode) * rows
            out_ref[mode, :, peer * width : (peer + 1) * width] = moved[at : at + rows]


def spread(order, values, firsts, seconds, place):
    peers, count, rows, _ = values[0].shape
    step = STEP
    width = place.shape[1]
    columns = peers * width
    return call(
        order,
        spread_body,
        (count // step,),
        [by_mode((peers, step, rows, v.shape[3]), 1) for v in values]
        + [whole(t.shape) for t in firsts + seconds]
        + [whole(place.shape)],
        [by_mode((step, rows, columns))],
        [jax.ShapeDtypeStruct((count, rows, columns), F32)],
        4 * count * rows * columns * width,
        8 * count * rows * columns,
        scratch=[pltpu.VMEM((8, width), F32)],
    )(*values, *firsts, *seconds, place)


def swap(value):
    return lax.all_to_all(value, "sz", split_axis=0, concat_axis=0, tiled=True)


def edges(first, last):
    peers = lax.axis_size("sx")
    up = [(i, (i + 1) % peers) for i in range(peers)]
    down = [(j, i) for i, j in up]
    return lax.ppermute(last, "sx", up), lax.ppermute(first, "sx", down)


def exchange(value, axis, distance):
    return lax.ppermute(value, axis, [(i, i ^ distance) for i in range(lax.axis_size(axis))])


def total_span(value):
    value = value + exchange(value, "sz", 1)
    return sum([exchange(value, "sz", d) for d in range(2, lax.axis_size("sz"), 2)], value)


def total_mode(value):
    distance = 1
    while distance < lax.axis_size("sx"):
        value = value + exchange(value, "sx", distance)
        distance *= 2
    return value


def wave_table(mode_count, span_count, amount):
    first_mode = lax.axis_index("sx") * mode_count
    first_span = lax.axis_index("sz") * span_count
    modes = first_mode + jnp.arange(mode_count, dtype=jnp.int32)
    spans = first_span + jnp.arange(span_count * amount, dtype=jnp.int32) // amount
    signed_x = jnp.where(modes < KX // 2, modes, modes - KX).astype(F32) * (4.0 / KX)
    signed_z = jnp.where(spans < KZ // 2, spans, spans - KZ).astype(F32) * (4.0 / KZ)
    return 1.0 + signed_x[:, None, None] ** 2 + signed_z[None, None, :] ** 2


class Chunk:
    def __init__(self, order, arrays, first, amount):
        self.order, self.amount = order, amount
        self.right_side, self.coupling, self.offsets, self.basis, self.inverse, self.size = arrays
        self.peers = lax.axis_size("sz")
        self.spans = KZ // self.peers
        self.pick = pick_matrix(self.spans, first, amount)
        self.wave = wave_table(self.right_side.shape[0], self.spans, amount)

    def send_high(self):
        self.high = swap(self.high)

    def send_low(self):
        self.low = swap(self.low)

    def gate_high(self):
        self.high = swap(gate(self.order, self.high))

    def gate_low(self):
        self.low = swap(gate(self.order, self.low))

    def begin(self):
        self.one, first, last, self.norm = begin(self.order, self.high, self.inverse, self.basis, self.size, self.wave)
        self.before, self.after = edges(first, last)

    def apply(self):
        self.image, self.sums = apply(
            self.order, self.offsets, self.before, self.one, self.after, self.coupling, self.wave, self.high
        )

    def rest(self):
        spans = total_span(rest(self.order, self.image, self.high, self.low, self.sums, self.norm))
        self.order.token = spans
        self.first = total_mode(spans)

    def again(self):
        self.residual, self.two, first, last, self.norm = again(
            self.order, self.amount, self.high, self.low, self.image, self.first, self.inverse, self.basis, self.size, self.wave
        )
        self.before, self.after = edges(first, last)

    def finish(self):
        sums = apply_last(
            self.order, self.offsets, self.before, self.two, self.after, self.coupling, self.wave, self.residual, self.norm
        )
        spans = total_span(sums)
        self.order.token = spans
        self.second = total_mode(spans)

    def combine(self):
        sent = combine(self.order, self.amount, self.one, self.two, self.first, self.second, self.peers)
        self.value = swap(sent.astype(jnp.float16)).astype(F32)


PLAN = (
    ("send_high", 0),
    ("send_low", 0),
    ("begin", 0),
    ("apply", 0),
    ("rest", 0),
    ("gate_high", 1),
    ("again", 0),
    ("finish", 0),
    ("gate_low", 1),
    ("begin", 1),
    ("apply", 1),
    ("rest", 1),
    ("combine", 0),
    ("again", 1),
    ("finish", 1),
    ("combine", 1),
)


def shards(right_side, coupling, offsets, basis, inverse, size):
    order = Order()
    arrays = (right_side, coupling, offsets, basis, inverse, size[:, None])
    chunks = [Chunk(order, arrays, first, amount) for first, amount in CHUNKS]
    peers = chunks[0].peers
    chunks[0].high, = pack(order, right_side, [chunks[0].pick], (0,), peers)
    others = [(chunks[0], 1)] + [(chunk, part) for chunk in chunks[1:] for part in (0, 1)]
    made = pack(order, right_side, [chunk.pick for chunk, _ in others], tuple(part for _, part in others), peers)
    for (chunk, part), value in zip(others, made):
        setattr(chunk, "low" if part else "high", value)
    for step, which in PLAN:
        getattr(chunks[which], step)()
    place = jnp.concatenate([c.pick.T for c in chunks], axis=0)
    return spread(order, [c.value for c in chunks], [c.first for c in chunks], [c.second for c in chunks], place)


def solution(mesh):
    in_specs = (P("sx", "sz", None), P("sx", None, None, None), P(), P(), P(), P())
    out_specs = P("sx", "sz", None)
    return jax.shard_map(shards, mesh=mesh, in_specs=in_specs, out_specs=out_specs, check_vma=False)
```

```python
import functools
import jax
import jax.numpy as jnp
from jax import lax
from jax.experimental import pallas as pl
from jax.experimental.pallas import tpu as pltpu
from jax.sharding import PartitionSpec as P

KX = 72
KZ = 128
H = 5
OFF = 6
R = 32
CHUNKS = ((0, 16), (16, 16))
F32 = jnp.float32
BF16 = jnp.bfloat16
TOP = 2.0**14
UNIT = 2.0**23
STEP = 3
VMEM = 24 * 2**20


class Order:
    def __init__(self):
        self.token = jnp.zeros((8, 128), F32)


def call(order, body, grid, in_specs, out_specs, out_shape, flops, moved, scratch=(), scalars=0):
    outs = len(out_shape)
    inputs = len(in_specs)

    def ordered(*refs):
        before, held, rest = refs[:scalars], refs[scalars : scalars + inputs], refs[scalars + inputs + 1 :]
        rest[outs][...] = jnp.zeros((8, 128), F32)
        body(*before, *held, *rest[:outs], *rest[outs + 1 :])

    kernel = pl.pallas_call(
        ordered,
        grid_spec=pltpu.PrefetchScalarGridSpec(
            num_scalar_prefetch=scalars,
            grid=grid,
            in_specs=in_specs + [pl.BlockSpec(memory_space=pl.ANY)],
            out_specs=out_specs + [whole((8, 128))],
            scratch_shapes=list(scratch),
        ),
        out_shape=out_shape + [jax.ShapeDtypeStruct((8, 128), F32)],
        compiler_params=pltpu.CompilerParams(vmem_limit_bytes=VMEM),
        cost_estimate=pl.CostEstimate(flops=int(flops), bytes_accessed=int(moved), transcendentals=0),
    )

    def run(*args):
        *given, order.token = kernel(*args, order.token)
        return given if outs > 1 else given[0]

    return run


def whole(shape):
    return pl.BlockSpec(shape, lambda m, *_: (0,) * len(shape))


def by_mode(shape, axis=0):
    return pl.BlockSpec(shape, lambda m, *_: (0,) * axis + (m,) + (0,) * (len(shape) - axis - 1))


def dot(a, b):
    return jnp.dot(a, b, preferred_element_type=F32)


def pack_body(parts, x_ref, *refs):
    picks, outs = refs[: len(parts)], refs[len(parts) :]
    modes, rows, columns = x_ref.shape
    width = picks[0].shape[0]
    peers = columns // width
    blocks = [x_ref[m, :, p * width : (p + 1) * width] for p in range(peers) for m in range(modes)]
    value = jnp.concatenate(blocks, axis=0)
    high = value.astype(BF16)
    if any(parts):
        wide = high.astype(F32)
        ratio = (value - wide) / jnp.where(wide == 0.0, 1.0, wide)
        code = jnp.clip(jnp.round(ratio * UNIT), -32767.0, 32767.0)
        upper = jnp.round(code * (1.0 / 256.0))
        lower = (code - upper * 256.0).astype(BF16)
        upper = upper.astype(BF16)
    for part, pick_ref, out_ref in zip(parts, picks, outs):
        if part:
            moved = dot(upper, pick_ref[...]) * 256.0 + dot(lower, pick_ref[...])
            moved = moved.astype(jnp.int32).astype(jnp.int16)
        else:
            moved = dot(high, pick_ref[...]).astype(BF16)
        for peer in range(peers):
            for mode in range(modes):
                at = (peer * modes + mode) * rows
                out_ref[peer, mode] = moved[at : at + rows]


def pack(order, right_side, picks, parts, peers):
    count, rows, columns = right_side.shape
    outs = [(peers, STEP, rows, pick.shape[1]) for pick in picks]
    kinds = [jnp.int16 if part else BF16 for part in parts]
    made = call(
        order,
        functools.partial(pack_body, parts),
        (count // STEP,),
        [by_mode((STEP, rows, columns))] + [whole(pick.shape) for pick in picks],
        [by_mode(shape, 1) for shape in outs],
        [jax.ShapeDtypeStruct((p, count, r, w), kind) for (p, _, r, w), kind in zip(outs, kinds)],
        2 * count * rows * columns * sum(pick.shape[1] * (1 + part) for pick, part in zip(picks, parts)),
        count * rows * columns * 4 + sum(2 * peers * count * rows * pick.shape[1] for pick in picks),
    )(right_side, *picks)
    return made if len(parts) > 1 else [made]


def pick_matrix(spans, first, amount):
    source = jnp.arange(spans * R, dtype=jnp.int32)[:, None]
    target = jnp.arange(spans * amount, dtype=jnp.int32)[None, :]
    wanted = (target // amount) * R + first + target % amount
    return (source == wanted).astype(BF16)


def gate_body(value_ref, token_ref, out_ref, next_ref):
    next_ref[...] = jnp.zeros((8, 128), F32)


def gate(order, value):
    far = pl.BlockSpec(memory_space=pl.ANY)
    value, order.token = pl.pallas_call(
        gate_body,
        in_specs=[far, far],
        out_specs=[far, pl.BlockSpec(memory_space=pltpu.VMEM)],
        out_shape=[jax.ShapeDtypeStruct(value.shape, value.dtype), jax.ShapeDtypeStruct((8, 128), F32)],
        input_output_aliases={0: 0},
    )(value, order.token)
    return value


def fold(payload, amount):
    width = payload.shape[1]
    row = lax.broadcasted_iota(jnp.int32, (width, width), 0)
    column = lax.broadcasted_iota(jnp.int32, (width, width), 1)
    same = ((row & (amount - 1)) == (column & (amount - 1))).astype(F32).astype(BF16)
    high = payload.astype(BF16)
    payload = payload - high.astype(F32)
    middle = payload.astype(BF16)
    low = (payload - middle.astype(F32)).astype(BF16)
    return dot(high, same) + (dot(middle, same) + dot(low, same))


def step_size(total):
    return total[0:1] / (total[1:2] + 1e-06)


def ceiling(first_total, second_total):
    reach = jnp.abs(step_size(first_total)) * jnp.sqrt(first_total[2:3])
    reach = reach + jnp.abs(step_size(second_total)) * jnp.sqrt(second_total[2:3])
    return jnp.maximum(jnp.max(reach, axis=1, keepdims=True), 1e-30)


def fold_rows(value):
    return jnp.sum(value.reshape(-1, 8, value.shape[-1]), axis=0)


def column_sum(value):
    return jnp.sum(value, axis=0, keepdims=True)


def is_first():
    return pl.program_id(0) == 0


def is_last():
    return pl.program_id(0) == pl.num_programs(0) - 1


def zero(ref):
    @pl.when(is_first())
    def _():
        ref[...] = jnp.zeros_like(ref)


def direction(rounded, wave, inverse_ref, basis_ref, size_ref):
    spectral = dot(inverse_ref[...], rounded)
    scaled = (spectral * (-1.0 / (size_ref[...] + wave))).astype(BF16)
    return dot(basis_ref[...], scaled).astype(BF16)


def hand_out(searches, search_ref, first_ref, last_ref, norm_ref, norm_scratch):
    at = pl.program_id(0)
    edge = OFF // STEP
    zero(norm_scratch)
    for i, search in enumerate(searches):
        search_ref[i] = search
        wide = search.astype(F32)
        norm_scratch[...] += fold_rows(wide * wide)

    @pl.when(at < edge)
    def _():
        for i, search in enumerate(searches):
            first_ref[i] = search

    @pl.when(at >= pl.num_programs(0) - edge)
    def _():
        for i, search in enumerate(searches):
            last_ref[i] = search

    @pl.when(is_last())
    def _():
        norm_ref[...] = norm_scratch[...]


def begin_body(high_ref, inverse_ref, basis_ref, size_ref, wave_ref, *outs):
    points = inverse_ref.shape[0]
    searches = []
    for i in range(STEP):
        rounded = high_ref[:, i].reshape(points, -1)
        searches.append(direction(rounded, wave_ref[i], inverse_ref, basis_ref, size_ref))
    hand_out(searches, *outs)


def edge_specs(count, points, width):
    shape = (STEP, points, width)
    edge = OFF // STEP
    first = pl.BlockSpec(shape, lambda m, *_: (jnp.minimum(m, edge - 1), 0, 0))
    last = pl.BlockSpec(shape, lambda m, *_: (jnp.maximum(m - (count // STEP - edge), 0), 0, 0))
    return [by_mode(shape), first, last, whole((8, width))]


def edge_shapes(count, points, width):
    shapes = [(count, points, width), (OFF, points, width), (OFF, points, width)]
    return [jax.ShapeDtypeStruct(s, BF16) for s in shapes] + [jax.ShapeDtypeStruct((8, width), F32)]


def begin(order, high, inverse, basis, size, wave):
    peers, count, rows, width = high.shape
    points = peers * rows
    return call(
        order,
        begin_body,
        (count // STEP,),
        [by_mode((peers, STEP, rows, width), 1), whole(inverse.shape), whole(basis.shape), whole(size.shape), by_mode((STEP, 1, width))],
        edge_specs(count, points, width),
        edge_shapes(count, points, width),
        4 * count * points * points * width,
        4 * count * points * width,
        scratch=[pltpu.VMEM((8, width), F32)],
    )(high, inverse, basis, size, wave)


def removed(high_ref, low_ref, i):
    high = high_ref[:, i].astype(F32)
    return (high * (1.0 / UNIT)) * low_ref[:, i].astype(jnp.int32).astype(F32)


def again_body(amount, high_ref, low_ref, image_ref, total_ref, inverse_ref, basis_ref, size_ref, wave_ref, residual_ref, *rest):
    outs, step_ref = rest[:-1], rest[-1]
    points = inverse_ref.shape[0]

    @pl.when(is_first())
    def _():
        step_ref[0:1] = step_size(fold(total_ref[...], amount))

    searches = []
    for i in range(STEP):
        held = high_ref[:, i].astype(F32) + removed(high_ref, low_ref, i)
        residual = held.reshape(points, -1) - step_ref[0:1] * image_ref[i]
        residual_ref[i] = residual
        searches.append(direction(residual.astype(BF16), wave_ref[i], inverse_ref, basis_ref, size_ref))
    hand_out(searches, *outs)


def again(order, amount, high, low, image, total, inverse, basis, size, wave):
    peers, count, rows, width = high.shape
    points = peers * rows
    block = by_mode((peers, STEP, rows, width), 1)
    plane = by_mode((STEP, points, width))
    return call(
        order,
        functools.partial(again_body, amount),
        (count // STEP,),
        [block, block, plane, whole(total.shape), whole(inverse.shape), whole(basis.shape), whole(size.shape), by_mode((STEP, 1, width))],
        [plane] + edge_specs(count, points, width),
        [jax.ShapeDtypeStruct((count, points, width), F32)] + edge_shapes(count, points, width),
        4 * count * points * points * width,
        14 * count * points * width,
        scratch=[pltpu.VMEM((8, width), F32), pltpu.VMEM((8, width), F32)],
    )(high, low, image, total, inverse, basis, size, wave)


def bring(before_ref, search_ref, after_ref, padded_ref, arrived):
    count = search_ref.shape[0]

    @pl.when(is_first())
    def _():
        parts = [
            pltpu.make_async_copy(before_ref, padded_ref.at[pl.ds(0, OFF)], arrived.at[0]),
            pltpu.make_async_copy(search_ref, padded_ref.at[pl.ds(OFF, count)], arrived.at[1]),
            pltpu.make_async_copy(after_ref, padded_ref.at[pl.ds(OFF + count, OFF)], arrived.at[2]),
        ]
        for part in parts:
            part.start()
        for part in parts:
            part.wait()


def operate(i, offsets_ref, coupling_ref, wave_ref, padded_ref):
    mode = pl.program_id(0) * STEP + i
    blocks = jnp.concatenate([coupling_ref[i, h] for h in range(H)], axis=1)
    sources = jnp.concatenate([padded_ref[mode + OFF + offsets_ref[h]] for h in range(H)], axis=0)
    return dot(blocks, sources) - wave_ref[i] * padded_ref[mode + OFF].astype(F32)


def apply_body(offsets_ref, before_ref, search_ref, after_ref, coupling_ref, wave_ref, high_ref, image_ref, sums_ref, padded_ref, arrived, sums):
    bring(before_ref, search_ref, after_ref, padded_ref, arrived)
    zero(sums)
    for i in range(STEP):
        image = operate(i, offsets_ref, coupling_ref, wave_ref, padded_ref)
        image_ref[i] = image
        sums[0:8] += fold_rows(image * high_ref[:, i].reshape(image.shape).astype(F32))
        sums[8:16] += fold_rows(image * image)

    @pl.when(is_last())
    def _():
        sums_ref[...] = jnp.zeros_like(sums_ref)
        sums_ref[0:1] = column_sum(sums[0:8])
        sums_ref[1:2] = column_sum(sums[8:16])


def apply_last_body(offsets_ref, before_ref, search_ref, after_ref, coupling_ref, wave_ref, residual_ref, norm_ref, sums_ref, padded_ref, arrived, sums):
    bring(before_ref, search_ref, after_ref, padded_ref, arrived)
    zero(sums)
    for i in range(STEP):
        image = operate(i, offsets_ref, coupling_ref, wave_ref, padded_ref)
        sums[0:8] += fold_rows(image * residual_ref[i])
        sums[8:16] += fold_rows(image * image)

    @pl.when(is_last())
    def _():
        sums_ref[...] = jnp.zeros_like(sums_ref)
        sums_ref[0:1] = column_sum(sums[0:8])
        sums_ref[1:2] = column_sum(sums[8:16])
        sums_ref[2:3] = column_sum(norm_ref[...])


def operator_specs(points, width):
    far = pl.BlockSpec(memory_space=pl.ANY)
    return [far, far, far, by_mode((STEP, H, points, points)), by_mode((STEP, 1, width))]


def operator_scratch(count, points, width):
    return [pltpu.VMEM((count + 2 * OFF, points, width), BF16), pltpu.SemaphoreType.DMA((3,)), pltpu.VMEM((16, width), F32)]


def apply(order, offsets, before, search, after, coupling, wave, high):
    count, points, width = search.shape
    peers, _, rows, _ = high.shape
    return call(
        order,
        apply_body,
        (count // STEP,),
        operator_specs(points, width) + [by_mode((peers, STEP, rows, width), 1)],
        [by_mode((STEP, points, width)), whole((8, width))],
        [jax.ShapeDtypeStruct((count, points, width), F32), jax.ShapeDtypeStruct((8, width), F32)],
        2 * H * count * points * points * width,
        2 * count * points * (H * points + 5 * width),
        scratch=operator_scratch(count, points, width),
        scalars=1,
    )(offsets, before, search, after, coupling, wave, high)


def apply_last(order, offsets, before, search, after, coupling, wave, residual, norm):
    count, points, width = search.shape
    return call(
        order,
        apply_last_body,
        (count // STEP,),
        operator_specs(points, width) + [by_mode((STEP, points, width)), whole(norm.shape)],
        [whole((8, width))],
        [jax.ShapeDtypeStruct((8, width), F32)],
        2 * H * count * points * points * width,
        2 * count * points * (H * points + 3 * width),
        scratch=operator_scratch(count, points, width),
        scalars=1,
    )(offsets, before, search, after, coupling, wave, residual, norm)


def rest_body(image_ref, high_ref, low_ref, sums_ref, norm_ref, out_ref, sums):
    zero(sums)
    for i in range(STEP):
        image = image_ref[i]
        sums[...] += fold_rows(image * removed(high_ref, low_ref, i).reshape(image.shape))

    @pl.when(is_last())
    def _():
        out_ref[...] = sums_ref[...]
        out_ref[0:1] += column_sum(sums[...])
        out_ref[2:3] = column_sum(norm_ref[...])


def rest(order, image, high, low, sums, norm):
    count, points, width = image.shape
    peers, _, rows, _ = low.shape
    return call(
        order,
        rest_body,
        (count // STEP,),
        [by_mode((STEP, points, width))] + [by_mode((peers, STEP, rows, width), 1)] * 2 + [whole(sums.shape), whole(norm.shape)],
        [whole((8, width))],
        [jax.ShapeDtypeStruct((8, width), F32)],
        2 * count * points * width,
        8 * count * points * width,
        scratch=[pltpu.VMEM((8, width), F32)],
    )(image, high, low, sums, norm)


def combine_body(amount, one_ref, two_ref, first_ref, second_ref, out_ref, step_ref):
    @pl.when(pl.program_id(0) == 0)
    def _():
        first_total = fold(first_ref[...], amount)
        second_total = fold(second_ref[...], amount)
        step_ref[0:1] = step_size(first_total)
        step_ref[1:2] = step_size(second_total)
        step_ref[2:3] = jnp.broadcast_to(TOP / ceiling(first_total, second_total), (1, step_ref.shape[1]))

    for i in range(STEP):
        value = step_ref[0:1] * one_ref[i].astype(F32) + step_ref[1:2] * two_ref[i].astype(F32)
        out_ref[:, i] = (value * step_ref[2:3]).reshape(out_ref.shape[0], out_ref.shape[2], -1)


def combine(order, amount, one, two, first_total, second_total, peers):
    count, points, width = one.shape
    rows = points // peers
    plane = by_mode((STEP, points, width))
    return call(
        order,
        functools.partial(combine_body, amount),
        (count // STEP,),
        [plane, plane, whole((8, width)), whole((8, width))],
        [by_mode((peers, STEP, rows, width), 1)],
        [jax.ShapeDtypeStruct((peers, count, rows, width), F32)],
        4 * count * points * width,
        8 * count * points * width,
        scratch=[pltpu.VMEM((8, width), F32)],
    )(one, two, first_total, second_total)


def spread_body(*refs):
    amounts = [amount for _, amount in CHUNKS]
    n = len(amounts)
    values, firsts, seconds = refs[:n], refs[n : 2 * n], refs[2 * n : 3 * n]
    place_ref, out_ref, scale_ref = refs[3 * n :]
    peers, modes, rows, _ = values[0].shape
    width = out_ref.shape[2] // peers

    @pl.when(pl.program_id(0) == 0)
    def _():
        side = lax.broadcasted_iota(jnp.int32, (1, width), 1) & (R - 1)
        scale = jnp.zeros((1, width), F32)
        for (first, amount), one_ref, two_ref in zip(CHUNKS, firsts, seconds):
            top = ceiling(fold(one_ref[...], amount), fold(two_ref[...], amount)) * (1.0 / TOP)
            scale = jnp.where((side >= first) & (side < first + amount), top, scale)
        scale_ref[0:1] = scale

    groups = min(v.shape[3] for v in values) // 128 or 1
    flat = [v[...].reshape(peers * modes * rows, v.shape[3]) for v in values]
    for group in range(groups):
        cuts = [v.shape[1] // groups for v in flat]
        joined = jnp.concatenate([v[:, group * cut : (group + 1) * cut] for v, cut in zip(flat, cuts)], axis=1)
        high = joined.astype(BF16)
        low = (joined - high.astype(F32)).astype(BF16)
        span = width // groups
        moved = dot(high, place_ref[...]) + dot(low, place_ref[...])
        moved = moved * scale_ref[0:1, group * span : (group + 1) * span]
        for peer in range(peers):
            for mode in range(modes):
                at = (peer * modes + mode) * rows
                left = peer * width + group * span
                out_ref[mode, :, left : left + span] = moved[at : at + rows]


def spread(order, values, firsts, seconds, place, spans):
    peers, count, rows, _ = values[0].shape
    step = STEP
    columns = peers * spans * R
    width = place.shape[1]
    return call(
        order,
        spread_body,
        (count // step,),
        [by_mode((peers, step, rows, v.shape[3]), 1) for v in values]
        + [whole(t.shape) for t in firsts + seconds]
        + [whole(place.shape)],
        [by_mode((step, rows, columns))],
        [jax.ShapeDtypeStruct((count, rows, columns), F32)],
        4 * count * rows * columns * width,
        8 * count * rows * columns,
        scratch=[pltpu.VMEM((8, spans * R), F32)],
    )(*values, *firsts, *seconds, place)


def swap(value):
    return lax.all_to_all(value, "sz", split_axis=0, concat_axis=0, tiled=True)


def edges(first, last):
    peers = lax.axis_size("sx")
    up = [(i, (i + 1) % peers) for i in range(peers)]
    down = [(j, i) for i, j in up]
    return lax.ppermute(last, "sx", up), lax.ppermute(first, "sx", down)


def exchange(value, axis, distance):
    return lax.ppermute(value, axis, [(i, i ^ distance) for i in range(lax.axis_size(axis))])


def total_span(value):
    value = value + exchange(value, "sz", 1)
    return sum([exchange(value, "sz", d) for d in range(2, lax.axis_size("sz"), 2)], value)


def total_mode(value):
    distance = 1
    while distance < lax.axis_size("sx"):
        value = value + exchange(value, "sx", distance)
        distance *= 2
    return value


def wave_table(mode_count, span_count, amount):
    first_mode = lax.axis_index("sx") * mode_count
    first_span = lax.axis_index("sz") * span_count
    modes = first_mode + jnp.arange(mode_count, dtype=jnp.int32)
    spans = first_span + jnp.arange(span_count * amount, dtype=jnp.int32) // amount
    signed_x = jnp.where(modes < KX // 2, modes, modes - KX).astype(F32) * (4.0 / KX)
    signed_z = jnp.where(spans < KZ // 2, spans, spans - KZ).astype(F32) * (4.0 / KZ)
    return 1.0 + signed_x[:, None, None] ** 2 + signed_z[None, None, :] ** 2


class Chunk:
    def __init__(self, order, arrays, first, amount):
        self.order, self.amount = order, amount
        self.right_side, self.coupling, self.offsets, self.basis, self.inverse, self.size = arrays
        self.peers = lax.axis_size("sz")
        self.spans = KZ // self.peers
        self.pick = pick_matrix(self.spans, first, amount)
        self.wave = wave_table(self.right_side.shape[0], self.spans, amount)

    def send_high(self):
        self.high = swap(self.high)

    def send_low(self):
        self.low = swap(self.low)

    def gate_high(self):
        self.high = swap(gate(self.order, self.high))

    def gate_low(self):
        self.low = swap(gate(self.order, self.low))

    def begin(self):
        self.one, first, last, self.norm = begin(self.order, self.high, self.inverse, self.basis, self.size, self.wave)
        self.before, self.after = edges(first, last)

    def apply(self):
        self.image, self.sums = apply(
            self.order, self.offsets, self.before, self.one, self.after, self.coupling, self.wave, self.high
        )

    def rest(self):
        spans = total_span(rest(self.order, self.image, self.high, self.low, self.sums, self.norm))
        self.order.token = spans
        self.first = total_mode(spans)

    def again(self):
        self.residual, self.two, first, last, self.norm = again(
            self.order, self.amount, self.high, self.low, self.image, self.first, self.inverse, self.basis, self.size, self.wave
        )
        self.before, self.after = edges(first, last)

    def settle(self):
        self.order.token = self.after

    def finish(self):
        sums = apply_last(
            self.order, self.offsets, self.before, self.two, self.after, self.coupling, self.wave, self.residual, self.norm
        )
        self.second = total_mode(total_span(sums))

    def combine(self):
        sent = combine(self.order, self.amount, self.one, self.two, self.first, self.second, self.peers)
        self.value = swap(sent.astype(jnp.float16)).astype(F32)


PLAN = (
    ("send_high", 0),
    ("send_low", 0),
    ("begin", 0),
    ("apply", 0),
    ("rest", 0),
    ("gate_high", 1),
    ("again", 0),
    ("settle", 0),
    ("gate_low", 1),
    ("begin", 1),
    ("finish", 0),
    ("apply", 1),
    ("rest", 1),
    ("combine", 0),
    ("again", 1),
    ("finish", 1),
    ("combine", 1),
)


def shards(right_side, coupling, offsets, basis, inverse, size):
    order = Order()
    arrays = (right_side, coupling, offsets, basis, inverse, size[:, None])
    chunks = [Chunk(order, arrays, first, amount) for first, amount in CHUNKS]
    peers = chunks[0].peers
    chunks[0].high, = pack(order, right_side, [chunks[0].pick], (0,), peers)
    others = [(chunks[0], 1)] + [(chunk, part) for chunk in chunks[1:] for part in (0, 1)]
    made = pack(order, right_side, [chunk.pick for chunk, _ in others], tuple(part for _, part in others), peers)
    for (chunk, part), value in zip(others, made):
        setattr(chunk, "low" if part else "high", value)
    for step, which in PLAN:
        getattr(chunks[which], step)()
    spans = chunks[0].spans
    groups = min(spans * amount for _, amount in CHUNKS) // 128 or 1
    place = jnp.concatenate([pick_matrix(spans // groups, *cut).T for cut in CHUNKS], axis=0)
    return spread(order, [c.value for c in chunks], [c.first for c in chunks], [c.second for c in chunks], place, spans)


def solution(mesh):
    in_specs = (P("sx", "sz", None), P("sx", None, None, None), P(), P(), P(), P())
    out_specs = P("sx", "sz", None)
    return jax.shard_map(shards, mesh=mesh, in_specs=in_specs, out_specs=out_specs, check_vma=False)
```
